32 devices in a mesh: groups: 2 (over x), tm: 16 (over z, y, core).
Axes of the slice: x: 2, y: 2, z: 4, core: 2. Of those that a mesh axis runs over, the one named last changes fastest.
Arguments:
- points: float32 [32, 64, 2048], P(('groups', 'tm')), parts along dimension 0, may hold values from -4 to 4
- potentials: float32 [32, 224, 2048], P(('groups', 'tm')), parts along dimension 0, may hold values from 0.5 to 25, as said below
- supports: int32 [32], P(('groups', 'tm')), parts along dimension 0, may hold values from 512 to 2048, as said below
Outputs:
- messages: float32 [32, 224, 2048], P(('groups', 'tm')), parts along dimension 0
- log_scale: float32 [448], P('groups'), parts along dimension 0
The draws below stay inside these ranges and needn't reach their ends.
There are 2 independent parts, one for each index of `groups`. The reference program is written for one: setup_inputs(seed, part) draws one part's arguments, and reference() takes and returns one part's arrays. A program takes and returns all parts, laid end to end along the dimension named above; each array names one. Nothing has to cross between parts.
Inputs may be any that keep to these rules, and one draw needn't show every extreme that they name: `supports`: the first and the last time slice have all 2048 points live; every other slice has between 512 and 1024 live points, at its first positions. `potentials`: positive scalings.
All inputs are finite; a program needn't handle non-finite values.
Results may differ from the reference program's by a relative error of at most 0.017.
Values may be sent and summed in bfloat16 or wider, within the bound.
A program may use at most 64 MiB of HBM per device.

```python
import jax
import jax.numpy as jnp
from jax import lax

DIM = 64
PTS = 2048
COLS = 224
SLICES = 16


def draw_points(key, part):
    first_key, second_key = jax.random.split(key, 2)
    start = jax.random.normal(first_key, (DIM, PTS), jnp.float32)
    innovations = 0.6 * jax.random.normal(second_key, (SLICES - 1, DIM, PTS), jnp.float32)
    start = jnp.clip(start, -4.0, 4.0)

    def advance(previous, innovation):
        following = jnp.clip(0.8 * previous + innovation, -4.0, 4.0)
        return (following, following)
    unused, later = lax.scan(advance, start, innovations)
    return jnp.concatenate([start[None], later], axis=0)


def draw_potentials(key, part):
    inner_key = jax.random.fold_in(key, 7)
    places = jnp.arange(SLICES).astype(jnp.float32) / (SLICES - 1)
    rough = jnp.exp(jax.random.uniform(inner_key, (SLICES, COLS, PTS), jnp.float32, -0.6931472, 0.6931472))
    growth = 1.5
    ramp = jnp.exp(growth * places)
    return rough * ramp[:, None, None]


def draw_supports(key, part):
    inner = jax.random.randint(key, (SLICES,), PTS // 4, PTS // 2 + 1)
    places = jnp.arange(SLICES)
    ends = (places == 0) | (places == SLICES - 1)
    return jnp.where(ends, PTS, inner).astype(jnp.int32)


def setup_inputs(seed: int = 0, part: int = 0) -> dict:
    arg_keys = jax.random.split(jax.random.key(seed), 4)
    part_keys = jax.random.split(jax.random.fold_in(arg_keys[3], part), 4)
    return {
        "points": draw_points(jax.random.fold_in(jax.random.fold_in(arg_keys[3], part), 71), part),
        "potentials": draw_potentials(jax.random.fold_in(jax.random.fold_in(arg_keys[3], part), 71), part),
        "supports": draw_supports(jax.random.fold_in(jax.random.fold_in(arg_keys[3], part), 71), part),
    }


A_DECAY = 0.8
EPS_SCALE = 0.05


def slice_kernel(source, target):
    dim_count, point_count = source.shape
    block_rows = min(512, point_count)
    inv_width = 1.0 / (2.0 * EPS_SCALE * dim_count)
    target_sq = jnp.sum(target * target, axis=0)
    pieces = jnp.transpose(source.reshape(dim_count, point_count // block_rows, block_rows), (1, 0, 2))

    def one_block(segment):
        products = lax.dot_general(segment, target, (((0,), (0,)), ((), ())), precision=lax.Precision.HIGHEST, preferred_element_type=jnp.float32)
        segment_sq = jnp.sum(segment * segment, axis=0)
        distance = target_sq[None, :] + (A_DECAY * A_DECAY) * segment_sq[:, None] - (2.0 * A_DECAY) * products
        return jnp.exp(-inv_width * distance).astype(jnp.bfloat16)

    return lax.map(one_block, pieces).reshape(point_count, point_count)


def reference(points, potentials, supports):
    slices, dim_count, point_count = points.shape
    live_mask = (jnp.arange(point_count)[None, :] < supports[:, None]).astype(jnp.float32)
    counts = supports.astype(jnp.float32)
    start_msg = jnp.broadcast_to(live_mask[0][None, :], (potentials.shape[1], point_count)).astype(jnp.float32)

    def advance(message, inputs):
        source, target, potential, live_row, support = inputs
        weighted = (message * potential).astype(jnp.bfloat16)
        kernel = slice_kernel(source, target)
        pushed = jnp.dot(weighted.astype(jnp.float32), kernel.astype(jnp.float32), precision=lax.Precision.HIGHEST, preferred_element_type=jnp.float32) * live_row[None, :]
        column_sum = jnp.sum(pushed, axis=1)
        following = pushed * (support / column_sum)[:, None]
        return following, (following, jnp.log(column_sum / support))

    unused, (later, log_terms) = lax.scan(advance, start_msg, (points[:-1], points[1:], potentials[:-1], live_mask[1:], counts[1:]))
    messages = jnp.concatenate([start_msg[None], later], axis=0)
    log_scale = jnp.sum(log_terms, axis=0) / (slices - 1)
    return messages, log_scale
```

```python
import functools
import math

import jax
import jax.numpy as jnp
from jax import lax
from jax.experimental import pallas as pl
from jax.experimental.pallas import tpu as pltpu
from jax.sharding import PartitionSpec as P

A_DECAY = 0.8
EPS_SCALE = 0.05
MESH = pl.DeviceIdType.MESH
F32 = jnp.float32
BF16 = jnp.bfloat16

TEAM = 4
ROWS = 64

R_PT, R_PRED, R_POT, R_G, R_W, R_LW, R_GA, R_LG, R_FIN = 0, 4, 5, 9, 13, 14, 15, 17, 21
N_RECV = 22
S_PT, S_PRED, S_POT, S_G, S_W, S_LW, S_GA, S_LG, S_W1, S_L1, S_FIN = 0, 3, 4, 7, 11, 12, 13, 16, 17, 20, 23


def split2(v):
    hi = v.astype(BF16)
    lo = (v - hi.astype(F32)).astype(BF16)
    return hi, lo


def split3(v):
    hi = v.astype(BF16)
    rest = v - hi.astype(F32)
    mid, lo = split2(rest)
    return hi.astype(F32), mid.astype(F32), lo.astype(F32)


def kernel(n_tm, starts, half, pts_in, pot_in, sup_in, out, logout,
           pts, pts2, potb, potb2, potr, kern, kern2, opa, opb, wbuf, w1, gat, gat2,
           push, logacc, log1, loggat, logfin, ssem, rsem):
    dim = pts_in.shape[1]
    cols = pot_in.shape[1]
    me = lax.axis_index("tm")
    q = lax.rem(me, TEAM)
    g = lax.div(me, TEAM)
    base = me - q
    n_g = n_tm // TEAM
    last = n_tm - 1
    sib = base + q + 1 - 2 * lax.rem(q, 2)
    yq = lax.rem(q + 2, TEAM)
    ymate = base + yq
    is_first = g == 0
    is_last = g == n_g - 1
    inner = jnp.logical_not(is_first)

    def rc(src, dst, s, r, dev):
        return pltpu.make_async_remote_copy(
            src_ref=src, dst_ref=dst, send_sem=ssem.at[s], recv_sem=rsem.at[r],
            device_id={"tm": dev}, device_id_type=MESH)

    def greet(dev):
        pl.semaphore_signal(barrier, inc=1, device_id={"tm": dev}, device_id_type=MESH)

    barrier = pltpu.get_barrier_semaphore()
    for d in range(1, TEAM):
        greet(base + lax.rem(q + d, TEAM))

    @pl.when(inner)
    def _():
        greet(me - TEAM)

    @pl.when(jnp.logical_not(is_last))
    def _():
        greet(me + TEAM)

    @pl.when(me != last)
    def _():
        greet(last)

    @pl.when(me == last)
    def _():
        for dev in range(n_tm - 1):
            greet(dev)

    support = sup_in[0]
    lane = lax.broadcasted_iota(jnp.int32, (8, half), 1)
    pts[q, 0:dim, :] = pts_in[0, :, 0:half]
    pts[q, dim:dim + 8, :] = (lane < support).astype(F32)
    pts2[0:dim, :] = pts_in[0, :, half:2 * half]
    pts2[dim:dim + 8, :] = (lane + half < support).astype(F32)
    for b in range(TEAM):
        potb[b] = pot_in[0, starts[b]:starts[b] + ROWS, 0:half].astype(BF16)

    @pl.when(me == 0)
    def _():
        for b in range(TEAM):
            potb2[b] = pot_in[0, starts[b]:starts[b] + ROWS, half:2 * half].astype(BF16)

    peers = (TEAM - 1 + jnp.where(is_first, 0, 1) + jnp.where(is_last, 0, 1)
             + jnp.where(me == last, n_tm - 1, 1))
    pl.semaphore_wait(barrier, peers)

    to_sib = rc(pts.at[q], pts.at[q], S_PT, R_PT + q, sib)
    to_ymate = rc(pts.at[q], pts.at[q], S_PT + 1, R_PT + q, ymate)
    to_sib.start()
    head = [rc(pts2, pts.at[TEAM], S_GA + 2, R_PRED, 1),
            rc(potb, gat, S_GA, R_GA, 1),
            rc(potb2, gat2, S_GA + 1, R_GA + 1, 1)]

    @pl.when(me == 0)
    def _():
        for c in head:
            c.start()

    to_ymate.start()
    sends_pot = jnp.logical_or(inner, q >= 2)
    pot_copies = []
    for d in range(1, TEAM):
        mq = lax.rem(q + d, TEAM)
        pot_copies.append(rc(potb.at[mq], potr.at[q], S_POT + d - 1, R_POT + q, base + mq))

    @pl.when(sends_pot)
    def _():
        for c in pot_copies:
            c.start()

    potr[q] = potb[q]

    def recv_points(slot):
        rc(pts.at[slot], pts.at[slot], S_PT, R_PT + slot, me).wait_recv()

    unit = math.log2(math.e) / (2.0 * EPS_SCALE * dim)

    def generate(src, dst, res):
        x = src[0:dim, :]
        y = dst[0:dim, :]
        live = dst[dim:dim + 1, :]
        u = (-unit * A_DECAY * A_DECAY) * jnp.sum(x * x, axis=0, keepdims=True)
        v = -unit * jnp.sum(y * y, axis=0, keepdims=True)
        v = jnp.where(live > 0.0, v, -1e9)
        row = lax.broadcasted_iota(jnp.int32, (dim, half), 0)
        uh, um, ul = split3(u)
        vh, vm, vl = split3(v)
        one = jnp.where(row < 6, 1.0, 0.0)
        xh, xl = split2(x)
        yh, yl = split2(y * (2.0 * A_DECAY * unit))
        opa[0:dim, :] = xh
        opa[dim:2 * dim, :] = xh
        opa[2 * dim:3 * dim, :] = xl
        opa[3 * dim:4 * dim, :] = jnp.where(
            row == 3, uh, jnp.where(row == 4, um, jnp.where(row == 5, ul, one))).astype(BF16)
        opb[0:dim, :] = yh
        opb[dim:2 * dim, :] = yl
        opb[2 * dim:3 * dim, :] = yh
        opb[3 * dim:4 * dim, :] = jnp.where(
            row == 0, vh, jnp.where(row == 1, vm, jnp.where(row == 2, vl, one))).astype(BF16)
        tile = 256

        @pl.loop(0, half // tile)
        def _(i):
            at = pl.ds(pl.multiple_of(i * tile, tile), tile)
            e = lax.dot_general(opa[:, at], opb[...], (((0,), (0,)), ((), ())),
                                preferred_element_type=F32)
            res[at, :] = jnp.exp2(e).astype(BF16)

    def log_row(value):
        spread = jnp.broadcast_to(value, (ROWS, 128))
        r0 = lax.broadcasted_iota(jnp.int32, (ROWS, 128), 0)
        r1 = lax.broadcasted_iota(jnp.int32, (ROWS, 128), 1)
        return jnp.sum(jnp.where(r0 == r1, spread, 0.0), axis=0, keepdims=True)

    def count(ref):
        return jnp.sum(ref[dim:dim + 1, :], axis=1, keepdims=True)

    def blocks(ref):
        return ref[...].reshape(TEAM * ROWS, half)

    w1_copies = []
    for d in range(1, TEAM):
        mq = lax.rem(1 + d, TEAM)
        w1_copies.append((rc(w1.at[mq], wbuf.at[2], S_W1 + d - 1, R_W, mq),
                          rc(log1.at[mq], logacc, S_L1 + d - 1, R_LW, mq)))

    recv_points(lax.rem(sib, TEAM))

    @pl.when(me == 1)
    def _():
        head[0].wait_recv()
        generate(pts.at[0], pts.at[1], kern.at[1])
        generate(pts.at[TEAM], pts.at[1], kern.at[0])
        head[1].wait_recv()
        head[2].wait_recv()
        pushed = (jnp.dot(blocks(gat), kern[1], preferred_element_type=F32)
                  + jnp.dot(blocks(gat2), kern[0], preferred_element_type=F32))
        cs = jnp.sum(pushed, axis=1, keepdims=True)
        cnt = count(pts.at[1])
        push[:, 0:half] = pushed * (cnt / cs)
        for b in (2, 3, 0, 1):
            rows = slice(starts[b], starts[b] + ROWS)
            m = push[b * ROWS:(b + 1) * ROWS, 0:half]
            w = (m * pot_in[0, rows, 0:half]).astype(BF16)
            if b == 1:
                wbuf[2] = w
            else:
                w1[b] = w
                w1_copies[(b + 2) % TEAM][0].start()
        for b in range(TEAM):
            lr = log_row(jnp.log(cs[b * ROWS:(b + 1) * ROWS] / cnt))
            if b == 1:
                logacc[...] = jnp.broadcast_to(lr, logacc.shape)
            else:
                log1[b] = jnp.broadcast_to(lr, logacc.shape)
                w1_copies[(b + 2) % TEAM][1].start()
        for b in range(TEAM):
            out[0, starts[b]:starts[b] + ROWS, 0:half] = push[b * ROWS:(b + 1) * ROWS, 0:half]

    recv_points(yq)
    forward = rc(pts.at[yq], pts.at[yq], S_PT + 2, R_PT + yq, sib)
    forward.start()
    recv_points(lax.rem(lax.rem(sib, TEAM) + 2, TEAM))
    pred = rc(pts.at[TEAM - 1], pts.at[TEAM], S_PRED, R_PRED, me + TEAM)

    @pl.when(jnp.logical_not(is_last))
    def _():
        pred.start()

    generate(pts.at[1], pts.at[2], kern.at[2])

    @pl.when(jnp.logical_or(jnp.logical_not(is_last), q == TEAM - 1))
    def _():
        generate(pts.at[2], pts.at[3], kern.at[3])

    @pl.when(me == last)
    def _():
        generate(pts.at[2], pts2, kern2)

    @pl.when(inner)
    def _():
        generate(pts.at[0], pts.at[1], kern.at[1])
        pred.wait_recv()
        generate(pts.at[TEAM], pts.at[0], kern.at[0])

    w_in = rc(wbuf.at[TEAM], wbuf.at[0], S_W, R_W, me + TEAM)
    l_in = rc(logacc, logacc, S_LW, R_LW, me + TEAM)

    @pl.when(me != 1)
    def _():
        w_in.wait_recv()
        l_in.wait_recv()

    to_owner = [rc(wbuf.at[s], gat.at[q], S_G + s, R_G + q, base + s) for s in range(TEAM)]

    def offer(s):
        @pl.when(q == s)
        def _():
            gat[q] = wbuf[s]

        @pl.when(q != s)
        def _():
            to_owner[s].start()

    def step(s):
        offer(s)
        pushed = jnp.dot(wbuf[s], kern[s], preferred_element_type=F32)
        cs = jnp.sum(pushed, axis=1, keepdims=True)
        cnt = count(pts.at[s])

        @pl.when(q != s)
        def _():
            rc(potr.at[s], potr.at[s], S_POT, R_POT + s, me).wait_recv()

        wbuf[s + 1] = (pushed * (cnt / cs) * potr[s].astype(F32)).astype(BF16)
        if s == TEAM - 1:
            w_in.start()
        logacc[...] += jnp.broadcast_to(log_row(jnp.log(cs / cnt)), logacc.shape)

    @pl.when(inner)
    def _():
        step(0)
        step(1)

    step(2)

    l_gat = rc(logacc, loggat.at[q], S_LG, R_LG + q, last)

    @pl.when(jnp.logical_not(is_last))
    def _():
        step(3)
        l_in.start()

    @pl.when(is_last)
    def _():
        offer(3)

        @pl.when(me != last)
        def _():
            l_gat.start()
            rc(potr.at[3], potr.at[3], S_POT, R_POT + 3, me).wait_recv()

        @pl.when(me == last)
        def _():
            loggat[q] = logacc[...]

    @pl.when(jnp.logical_or(inner, q >= 2))
    def _():
        for d in range(1, TEAM):
            mq = lax.rem(q + d, TEAM)
            rc(gat.at[mq], gat.at[mq], S_G, R_G + mq, me).wait_recv()

    @pl.when(me == 0)
    def _():
        full = lax.broadcasted_iota(jnp.int32, (cols, 2 * half), 1)
        out[0] = (full < support).astype(F32)

    @pl.when(jnp.logical_and(me != 0, me != last))
    def _():
        out[0, :, half:2 * half] = jnp.zeros((cols, half), F32)

    @pl.when(jnp.logical_and(jnp.logical_or(inner, q >= 2), me != last))
    def _():
        pushed = jnp.dot(blocks(gat), kern[q], preferred_element_type=F32)
        cs = jnp.sum(pushed, axis=1, keepdims=True)
        push[:, 0:half] = pushed * (count(pts.at[q]) / cs)
        for b in range(TEAM):
            out[0, starts[b]:starts[b] + ROWS, 0:half] = push[b * ROWS:(b + 1) * ROWS, 0:half]

    fin = [rc(logfin, logfin, S_FIN + dev, R_FIN, dev) for dev in range(n_tm - 1)]

    @pl.when(me == last)
    def _():
        pa = jnp.dot(blocks(gat), kern[TEAM - 1], preferred_element_type=F32)
        pb = jnp.dot(blocks(gat), kern2[...], preferred_element_type=F32)
        cs = jnp.sum(pa, axis=1, keepdims=True) + jnp.sum(pb, axis=1, keepdims=True)
        cnt = count(pts.at[TEAM - 1]) + count(pts2)
        term = jnp.log(cs / cnt)
        for b in range(TEAM - 1):
            rc(loggat.at[b], loggat.at[b], S_LG, R_LG + b, me).wait_recv()
        logfin[...] = jnp.zeros_like(logfin)
        for b in range(TEAM):
            total = loggat[b, 0:1, :] + log_row(term[b * ROWS:(b + 1) * ROWS])
            logfin[b:b + 1, :] = total * (1.0 / (n_tm - 1))
        for c in fin:
            c.start()
        push[:, 0:half] = pa * (cnt / cs)
        push[:, half:2 * half] = pb * (cnt / cs)
        for b in range(TEAM):
            out[0, starts[b]:starts[b] + ROWS, :] = push[b * ROWS:(b + 1) * ROWS, :]
        for c in fin:
            c.wait_send()

    to_sib.wait_send()
    to_ymate.wait_send()
    forward.wait_send()

    @pl.when(me == 0)
    def _():
        for c in head:
            c.wait_send()

    @pl.when(me == 1)
    def _():
        for a, b in w1_copies:
            a.wait_send()
            b.wait_send()

    @pl.when(sends_pot)
    def _():
        for c in pot_copies:
            c.wait_send()

    @pl.when(jnp.logical_not(is_last))
    def _():
        pred.wait_send()
        w_in.wait_send()
        l_in.wait_send()

    for s in range(TEAM):
        sent = jnp.logical_and(q != s, jnp.logical_or(inner, s >= 2))

        @pl.when(sent)
        def _(s=s):
            to_owner[s].wait_send()

    @pl.when(jnp.logical_and(is_last, me != last))
    def _():
        l_gat.wait_send()

    @pl.when(me != last)
    def _():
        rc(logfin, logfin, S_FIN, R_FIN, me).wait_recv()

    logout[...] = logfin[...]


def per_device(n_tm, points, potentials, supports):
    slices, dim, count = points.shape
    cols = potentials.shape[1]
    half = count // 2
    starts = [(b * (cols - ROWS) // (TEAM - 1)) // 16 * 16 for b in range(TEAM)]
    vm = lambda shape, dtype: pltpu.VMEM(shape, dtype)
    messages, logs = pl.pallas_call(
        functools.partial(kernel, n_tm, starts, half),
        out_shape=(jax.ShapeDtypeStruct((slices, cols, count), F32),
                   jax.ShapeDtypeStruct((8, 128), F32)),
        in_specs=[pl.BlockSpec(memory_space=pltpu.VMEM),
                  pl.BlockSpec(memory_space=pltpu.VMEM),
                  pl.BlockSpec(memory_space=pltpu.SMEM)],
        out_specs=(pl.BlockSpec(memory_space=pltpu.VMEM),
                   pl.BlockSpec(memory_space=pltpu.VMEM)),
        scratch_shapes=[
            vm((TEAM + 1, dim + 8, half), F32),
            vm((dim + 8, half), F32),
            vm((TEAM, ROWS, half), BF16),
            vm((TEAM, ROWS, half), BF16),
            vm((TEAM, ROWS, half), BF16),
            vm((TEAM, half, half), BF16),
            vm((half, half), BF16),
            vm((4 * dim, half), BF16),
            vm((4 * dim, half), BF16),
            vm((TEAM + 1, ROWS, half), BF16),
            vm((TEAM, ROWS, half), BF16),
            vm((TEAM, ROWS, half), BF16),
            vm((TEAM, ROWS, half), BF16),
            vm((TEAM * ROWS, 2 * half), F32),
            vm((8, 128), F32),
            vm((TEAM, 8, 128), F32),
            vm((TEAM, 8, 128), F32),
            vm((8, 128), F32),
            pltpu.SemaphoreType.DMA((S_FIN + n_tm,)),
            pltpu.SemaphoreType.DMA((N_RECV,)),
        ],
        compiler_params=pltpu.CompilerParams(
            collective_id=0, has_side_effects=True, vmem_limit_bytes=48 * 1024 * 1024),
    )(points, potentials, supports)
    ends = starts[1:] + [cols]
    log_scale = jnp.concatenate(
        [logs[b, 0:ends[b] - starts[b]] for b in range(TEAM)])
    return messages, log_scale


def solution(mesh):
    placed = (P(("groups", "tm"), None, None), P(("groups", "tm"), None, None), P(("groups", "tm")))
    return jax.shard_map(
        functools.partial(per_device, mesh.shape["tm"]),
        mesh=mesh,
        in_specs=placed,
        out_specs=(P(("groups", "tm"), None, None), P("groups")),
        check_vma=False,
    )
```

```python
import functools
import math

import jax
import jax.numpy as jnp
from jax import lax
from jax.experimental import pallas as pl
from jax.experimental.pallas import tpu as pltpu
from jax.sharding import PartitionSpec as P

A_DECAY = 0.8
EPS_SCALE = 0.05
MESH = pl.DeviceIdType.MESH
F32 = jnp.float32
BF16 = jnp.bfloat16

TEAM = 4
ROWS = 64

R_PT, R_PRED, R_POT, R_G, R_W, R_LW, R_GA, R_LG, R_FIN = 0, 4, 5, 9, 13, 14, 15, 17, 21
N_RECV = 22
S_PT, S_PRED, S_POT, S_G, S_W, S_LW, S_GA, S_LG, S_W1, S_L1, S_FIN = 0, 3, 4, 7, 11, 12, 13, 16, 17, 20, 23


def split2(v):
    hi = v.astype(BF16)
    lo = (v - hi.astype(F32)).astype(BF16)
    return hi, lo


def split3(v):
    hi = v.astype(BF16)
    rest = v - hi.astype(F32)
    mid, lo = split2(rest)
    return hi.astype(F32), mid.astype(F32), lo.astype(F32)


def kernel(n_tm, starts, half, pts_hbm, pot_hbm, sup_in, out, logout,
           pts, pts2, potb, potb2, potr, kern, kern2, opa, opb, wbuf, w1, gat, gat2,
           push, logacc, log1, loggat, logfin, pot_in, ssem, rsem, lsem):
    dim = pts_hbm.shape[1]
    cols = pot_hbm.shape[1]
    me = lax.axis_index("tm")
    q = lax.rem(me, TEAM)
    g = lax.div(me, TEAM)
    base = me - q
    n_g = n_tm // TEAM
    last = n_tm - 1
    sib = base + q + 1 - 2 * lax.rem(q, 2)
    yq = lax.rem(q + 2, TEAM)
    ymate = base + yq
    is_first = g == 0
    is_last = g == n_g - 1
    inner = jnp.logical_not(is_first)

    def rc(src, dst, s, r, dev):
        return pltpu.make_async_remote_copy(
            src_ref=src, dst_ref=dst, send_sem=ssem.at[s], recv_sem=rsem.at[r],
            device_id={"tm": dev}, device_id_type=MESH)

    def greet(dev):
        pl.semaphore_signal(barrier, inc=1, device_id={"tm": dev}, device_id_type=MESH)

    barrier = pltpu.get_barrier_semaphore()
    for d in range(1, TEAM):
        greet(base + lax.rem(q + d, TEAM))

    @pl.when(inner)
    def _():
        greet(me - TEAM)

    @pl.when(jnp.logical_not(is_last))
    def _():
        greet(me + TEAM)

    @pl.when(me != last)
    def _():
        greet(last)

    @pl.when(me == last)
    def _():
        for dev in range(n_tm - 1):
            greet(dev)

    support = sup_in[0]
    lane = lax.broadcasted_iota(jnp.int32, (8, half), 1)
    loads = [pltpu.make_async_copy(pts_hbm.at[0, :, 0:half], pts.at[q, 0:dim], lsem.at[0]),
             pltpu.make_async_copy(pts_hbm.at[0, :, half:2 * half], pts2.at[0:dim], lsem.at[1]),
             pltpu.make_async_copy(pot_hbm, pot_in, lsem.at[2])]
    for c in loads:
        c.start()
    pts[q, dim:dim + 8, :] = (lane < support).astype(F32)
    pts2[dim:dim + 8, :] = (lane + half < support).astype(F32)
    loads[0].wait()
    loads[1].wait()
    peers = (TEAM - 1 + jnp.where(is_first, 0, 1) + jnp.where(is_last, 0, 1)
             + jnp.where(me == last, n_tm - 1, 1))
    pl.semaphore_wait(barrier, peers)

    to_sib = rc(pts.at[q], pts.at[q], S_PT, R_PT + q, sib)
    to_ymate = rc(pts.at[q], pts.at[q], S_PT + 1, R_PT + q, ymate)
    to_sib.start()
    head = [rc(pts2, pts.at[TEAM], S_GA + 2, R_PRED, 1),
            rc(potb, gat, S_GA, R_GA, 1),
            rc(potb2, gat2, S_GA + 1, R_GA + 1, 1)]

    @pl.when(me == 0)
    def _():
        head[0].start()

    @pl.when(me != 0)
    def _():
        to_ymate.start()

    loads[2].wait()
    for b in range(TEAM):
        potb[b] = pot_in[0, starts[b]:starts[b] + ROWS, 0:half].astype(BF16)

    @pl.when(me == 0)
    def _():
        for b in range(TEAM):
            potb2[b] = pot_in[0, starts[b]:starts[b] + ROWS, half:2 * half].astype(BF16)

    @pl.when(me == 0)
    def _():
        head[1].start()
        head[2].start()

    sends_pot = jnp.logical_or(inner, q >= 2)
    pot_copies = []
    for d in range(1, TEAM):
        mq = lax.rem(q + d, TEAM)
        pot_copies.append(rc(potb.at[mq], potr.at[q], S_POT + d - 1, R_POT + q, base + mq))

    @pl.when(sends_pot)
    def _():
        for c in pot_copies:
            c.start()

    potr[q] = potb[q]

    def recv_points(slot):
        rc(pts.at[slot], pts.at[slot], S_PT, R_PT + slot, me).wait_recv()

    unit = math.log2(math.e) / (2.0 * EPS_SCALE * dim)

    def generate(src, dst, res):
        x = src[0:dim, :]
        y = dst[0:dim, :]
        live = dst[dim:dim + 1, :]
        u = (-unit * A_DECAY * A_DECAY) * jnp.sum(x * x, axis=0, keepdims=True)
        v = -unit * jnp.sum(y * y, axis=0, keepdims=True)
        v = jnp.where(live > 0.0, v, -1e9)
        row = lax.broadcasted_iota(jnp.int32, (dim, half), 0)
        uh, um, ul = split3(u)
        vh, vm, vl = split3(v)
        one = jnp.where(row < 6, 1.0, 0.0)
        xh, xl = split2(x)
        yh, yl = split2(y * (2.0 * A_DECAY * unit))
        opa[0:dim, :] = xh
        opa[dim:2 * dim, :] = xh
        opa[2 * dim:3 * dim, :] = xl
        opa[3 * dim:4 * dim, :] = jnp.where(
            row == 3, uh, jnp.where(row == 4, um, jnp.where(row == 5, ul, one))).astype(BF16)
        opb[0:dim, :] = yh
        opb[dim:2 * dim, :] = yl
        opb[2 * dim:3 * dim, :] = yh
        opb[3 * dim:4 * dim, :] = jnp.where(
            row == 0, vh, jnp.where(row == 1, vm, jnp.where(row == 2, vl, one))).astype(BF16)
        tile = 256

        @pl.loop(0, half // tile)
        def _(i):
            at = pl.ds(pl.multiple_of(i * tile, tile), tile)
            e = lax.dot_general(opa[:, at], opb[...], (((0,), (0,)), ((), ())),
                                preferred_element_type=F32)
            res[at, :] = jnp.exp2(e).astype(BF16)

    def log_row(value):
        spread = jnp.broadcast_to(value, (ROWS, 128))
        r0 = lax.broadcasted_iota(jnp.int32, (ROWS, 128), 0)
        r1 = lax.broadcasted_iota(jnp.int32, (ROWS, 128), 1)
        return jnp.sum(jnp.where(r0 == r1, spread, 0.0), axis=0, keepdims=True)

    def count(ref):
        return jnp.sum(ref[dim:dim + 1, :], axis=1, keepdims=True)

    def blocks(ref):
        return ref[...].reshape(TEAM * ROWS, half)

    w1_copies = []
    for d in range(1, TEAM):
        mq = lax.rem(1 + d, TEAM)
        w1_copies.append((rc(w1.at[mq], wbuf.at[2], S_W1 + d - 1, R_W, mq),
                          rc(log1.at[mq], logacc, S_L1 + d - 1, R_LW, mq)))

    recv_points(lax.rem(sib, TEAM))

    @pl.when(me == 1)
    def _():
        head[0].wait_recv()
        generate(pts.at[0], pts.at[1], kern.at[1])
        generate(pts.at[TEAM], pts.at[1], kern.at[0])
        head[1].wait_recv()
        head[2].wait_recv()
        pushed = (jnp.dot(blocks(gat), kern[1], preferred_element_type=F32)
                  + jnp.dot(blocks(gat2), kern[0], preferred_element_type=F32))
        cs = jnp.sum(pushed, axis=1, keepdims=True)
        cnt = count(pts.at[1])
        push[:, 0:half] = pushed * (cnt / cs)
        for b in (2, 3, 0, 1):
            rows = slice(starts[b], starts[b] + ROWS)
            m = push[b * ROWS:(b + 1) * ROWS, 0:half]
            w = (m * pot_in[0, rows, 0:half]).astype(BF16)
            if b == 1:
                wbuf[2] = w
            else:
                w1[b] = w
                w1_copies[(b + 2) % TEAM][0].start()
        for b in range(TEAM):
            lr = log_row(jnp.log(cs[b * ROWS:(b + 1) * ROWS] / cnt))
            if b == 1:
                logacc[...] = jnp.broadcast_to(lr, logacc.shape)
            else:
                log1[b] = jnp.broadcast_to(lr, logacc.shape)
                w1_copies[(b + 2) % TEAM][1].start()
        for b in range(TEAM):
            out[0, starts[b]:starts[b] + ROWS, 0:half] = push[b * ROWS:(b + 1) * ROWS, 0:half]

    forward = rc(pts.at[yq], pts.at[yq], S_PT + 2, R_PT + yq, sib)
    diag = lax.rem(lax.rem(sib, TEAM) + 2, TEAM)

    @pl.when(me != 2)
    def _():
        recv_points(yq)
        forward.start()

    @pl.when(me != 3)
    def _():
        recv_points(diag)

    pred = rc(pts.at[TEAM - 1], pts.at[TEAM], S_PRED, R_PRED, me + TEAM)

    @pl.when(jnp.logical_not(is_last))
    def _():
        pred.start()

    generate(pts.at[1], pts.at[2], kern.at[2])

    @pl.when(jnp.logical_or(jnp.logical_not(is_last), q == TEAM - 1))
    def _():
        generate(pts.at[2], pts.at[3], kern.at[3])

    @pl.when(me == last)
    def _():
        generate(pts.at[2], pts2, kern2)

    @pl.when(inner)
    def _():
        generate(pts.at[0], pts.at[1], kern.at[1])
        pred.wait_recv()
        generate(pts.at[TEAM], pts.at[0], kern.at[0])

    w_in = rc(wbuf.at[TEAM], wbuf.at[0], S_W, R_W, me + TEAM)
    l_in = rc(logacc, logacc, S_LW, R_LW, me + TEAM)

    @pl.when(me != 1)
    def _():
        w_in.wait_recv()
        l_in.wait_recv()

    to_owner = [rc(wbuf.at[s], gat.at[q], S_G + s, R_G + q, base + s) for s in range(TEAM)]

    def offer(s):
        @pl.when(q == s)
        def _():
            gat[q] = wbuf[s]

        @pl.when(q != s)
        def _():
            to_owner[s].start()

    def step(s):
        if s == 2:
            @pl.when(jnp.logical_not(is_last))
            def _():
                offer(s)
        else:
            offer(s)

        pushed = jnp.dot(wbuf[s], kern[s], preferred_element_type=F32)
        cs = jnp.sum(pushed, axis=1, keepdims=True)
        cnt = count(pts.at[s])

        @pl.when(q != s)
        def _():
            rc(potr.at[s], potr.at[s], S_POT, R_POT + s, me).wait_recv()

        wbuf[s + 1] = (pushed * (cnt / cs) * potr[s].astype(F32)).astype(BF16)
        if s == TEAM - 1:
            w_in.start()
        logacc[...] += jnp.broadcast_to(log_row(jnp.log(cs / cnt)), logacc.shape)

    @pl.when(inner)
    def _():
        step(0)
        step(1)

    step(2)

    l_gat = rc(logacc, loggat.at[q], S_LG, R_LG + q, last)

    @pl.when(jnp.logical_not(is_last))
    def _():
        step(3)
        l_in.start()

    @pl.when(is_last)
    def _():
        offer(3)

        @pl.when(me != last)
        def _():
            l_gat.start()
            to_owner[3].wait_send()

        offer(2)

        @pl.when(me != last)
        def _():
            rc(potr.at[3], potr.at[3], S_POT, R_POT + 3, me).wait_recv()

        @pl.when(me == last)
        def _():
            loggat[q] = logacc[...]

    @pl.when(jnp.logical_or(inner, q >= 2))
    def _():
        for d in range(1, TEAM):
            mq = lax.rem(q + d, TEAM)
            rc(gat.at[mq], gat.at[mq], S_G, R_G + mq, me).wait_recv()

    @pl.when(me == 0)
    def _():
        full = lax.broadcasted_iota(jnp.int32, (cols, 2 * half), 1)
        out[0] = (full < support).astype(F32)

    @pl.when(jnp.logical_and(me != 0, me != last))
    def _():
        out[0, :, half:2 * half] = jnp.zeros((cols, half), F32)

    @pl.when(jnp.logical_and(jnp.logical_or(inner, q >= 2), me != last))
    def _():
        pushed = jnp.dot(blocks(gat), kern[q], preferred_element_type=F32)
        cs = jnp.sum(pushed, axis=1, keepdims=True)
        push[:, 0:half] = pushed * (count(pts.at[q]) / cs)
        for b in range(TEAM):
            out[0, starts[b]:starts[b] + ROWS, 0:half] = push[b * ROWS:(b + 1) * ROWS, 0:half]

    fin = [rc(logfin, logfin, S_FIN + dev, R_FIN, dev) for dev in range(n_tm - 1)]

    @pl.when(me == last)
    def _():
        pa = jnp.dot(blocks(gat), kern[TEAM - 1], preferred_element_type=F32)
        pb = jnp.dot(blocks(gat), kern2[...], preferred_element_type=F32)
        cs = jnp.sum(pa, axis=1, keepdims=True) + jnp.sum(pb, axis=1, keepdims=True)
        cnt = count(pts.at[TEAM - 1]) + count(pts2)
        term = jnp.log(cs / cnt)
        for b in range(TEAM - 1):
            rc(loggat.at[b], loggat.at[b], S_LG, R_LG + b, me).wait_recv()
        logfin[...] = jnp.zeros_like(logfin)
        for b in range(TEAM):
            total = loggat[b, 0:1, :] + log_row(term[b * ROWS:(b + 1) * ROWS])
            logfin[b:b + 1, :] = total * (1.0 / (n_tm - 1))
        for c in fin:
            c.start()
        push[:, 0:half] = pa * (cnt / cs)
        push[:, half:2 * half] = pb * (cnt / cs)
        for b in range(TEAM):
            out[0, starts[b]:starts[b] + ROWS, :] = push[b * ROWS:(b + 1) * ROWS, :]
        for c in fin:
            c.wait_send()

    to_sib.wait_send()

    @pl.when(me != 0)
    def _():
        to_ymate.wait_send()

    @pl.when(me != 2)
    def _():
        forward.wait_send()

    @pl.when(me == 0)
    def _():
        for c in head:
            c.wait_send()

    @pl.when(me == 1)
    def _():
        for a, b in w1_copies:
            a.wait_send()
            b.wait_send()

    @pl.when(sends_pot)
    def _():
        for c in pot_copies:
            c.wait_send()

    @pl.when(jnp.logical_not(is_last))
    def _():
        pred.wait_send()
        w_in.wait_send()
        l_in.wait_send()

    for s in range(TEAM):
        sent = jnp.logical_and(q != s, jnp.logical_or(inner, s >= 2))
        if s == 3:
            sent = jnp.logical_and(sent, jnp.logical_not(is_last))

        @pl.when(sent)
        def _(s=s):
            to_owner[s].wait_send()

    @pl.when(jnp.logical_and(is_last, me != last))
    def _():
        l_gat.wait_send()

    @pl.when(me != last)
    def _():
        rc(logfin, logfin, S_FIN, R_FIN, me).wait_recv()

    logout[...] = logfin[...]


def per_device(n_tm, points, potentials, supports):
    slices, dim, count = points.shape
    cols = potentials.shape[1]
    half = count // 2
    starts = [(b * (cols - ROWS) // (TEAM - 1)) // 16 * 16 for b in range(TEAM)]
    vm = lambda shape, dtype: pltpu.VMEM(shape, dtype)
    messages, logs = pl.pallas_call(
        functools.partial(kernel, n_tm, starts, half),
        out_shape=(jax.ShapeDtypeStruct((slices, cols, count), F32),
                   jax.ShapeDtypeStruct((8, 128), F32)),
        in_specs=[pl.BlockSpec(memory_space=pltpu.HBM),
                  pl.BlockSpec(memory_space=pltpu.HBM),
                  pl.BlockSpec(memory_space=pltpu.SMEM)],
        out_specs=(pl.BlockSpec(memory_space=pltpu.VMEM),
                   pl.BlockSpec(memory_space=pltpu.VMEM)),
        scratch_shapes=[
            vm((TEAM + 1, dim + 8, half), F32),
            vm((dim + 8, half), F32),
            vm((TEAM, ROWS, half), BF16),
            vm((TEAM, ROWS, half), BF16),
            vm((TEAM, ROWS, half), BF16),
            vm((TEAM, half, half), BF16),
            vm((half, half), BF16),
            vm((4 * dim, half), BF16),
            vm((4 * dim, half), BF16),
            vm((TEAM + 1, ROWS, half), BF16),
            vm((TEAM, ROWS, half), BF16),
            vm((TEAM, ROWS, half), BF16),
            vm((TEAM, ROWS, half), BF16),
            vm((TEAM * ROWS, 2 * half), F32),
            vm((8, 128), F32),
            vm((TEAM, 8, 128), F32),
            vm((TEAM, 8, 128), F32),
            vm((8, 128), F32),
            vm((slices, cols, count), F32),
            pltpu.SemaphoreType.DMA((S_FIN + n_tm,)),
            pltpu.SemaphoreType.DMA((N_RECV,)),
            pltpu.SemaphoreType.DMA((3,)),
        ],
        compiler_params=pltpu.CompilerParams(
            collective_id=0, has_side_effects=True, vmem_limit_bytes=48 * 1024 * 1024),
    )(points, potentials, supports)
    ends = starts[1:] + [cols]
    log_scale = jnp.concatenate(
        [logs[b, 0:ends[b] - starts[b]] for b in range(TEAM)])
    return messages, log_scale


def solution(mesh):
    placed = (P(("groups", "tm"), None, None), P(("groups", "tm"), None, None), P(("groups", "tm")))
    return jax.shard_map(
        functools.partial(per_device, mesh.shape["tm"]),
        mesh=mesh,
        in_specs=placed,
        out_specs=(P(("groups", "tm"), None, None), P("groups")),
        check_vma=False,
    )
```

```python
import functools
import math

import jax
import jax.numpy as jnp
from jax import lax
from jax.experimental import pallas as pl
from jax.experimental.pallas import tpu as pltpu
from jax.sharding import PartitionSpec as P

A_DECAY = 0.8
EPS_SCALE = 0.05
MESH = pl.DeviceIdType.MESH
F32 = jnp.float32
BF16 = jnp.bfloat16

TEAM = 4
ROWS = 64

R_PT, R_PRED, R_POT, R_G, R_W, R_LW, R_GA, R_LG, R_FIN = 0, 4, 5, 9, 13, 14, 15, 17, 21
N_RECV = 22
S_PT, S_PRED, S_POT, S_G, S_W, S_LW, S_GA, S_LG, S_W1, S_L1, S_FIN = 0, 3, 4, 7, 11, 12, 13, 16, 17, 20, 23


def split2(v):
    hi = v.astype(BF16)
    lo = (v - hi.astype(F32)).astype(BF16)
    return hi, lo


def split3(v):
    hi = v.astype(BF16)
    rest = v - hi.astype(F32)
    mid, lo = split2(rest)
    return hi.astype(F32), mid.astype(F32), lo.astype(F32)


def kernel(n_tm, starts, half, pts_hbm, pot_hbm, sup_in, out, logout,
           pts, pts2, potb, potb2, potr, kern, kern2, opa, opb, wbuf, w1, gat, gat2,
           push, logacc, log1, loggat, logfin, pot_in, ssem, rsem, lsem):
    dim = pts_hbm.shape[1]
    cols = pot_hbm.shape[1]
    me = lax.axis_index("tm")
    q = lax.rem(me, TEAM)
    g = lax.div(me, TEAM)
    base = me - q
    n_g = n_tm // TEAM
    last = n_tm - 1
    sib = base + q + 1 - 2 * lax.rem(q, 2)
    yq = lax.rem(q + 2, TEAM)
    ymate = base + yq
    is_first = g == 0
    is_last = g == n_g - 1
    inner = jnp.logical_not(is_first)

    def rc(src, dst, s, r, dev):
        return pltpu.make_async_remote_copy(
            src_ref=src, dst_ref=dst, send_sem=ssem.at[s], recv_sem=rsem.at[r],
            device_id={"tm": dev}, device_id_type=MESH)

    def greet(dev):
        pl.semaphore_signal(barrier, inc=1, device_id={"tm": dev}, device_id_type=MESH)

    barrier = pltpu.get_barrier_semaphore()
    for d in range(1, TEAM):
        greet(base + lax.rem(q + d, TEAM))

    @pl.when(inner)
    def _():
        greet(me - TEAM)

    @pl.when(jnp.logical_not(is_last))
    def _():
        greet(me + TEAM)

    @pl.when(me != last)
    def _():
        greet(last)

    @pl.when(me == last)
    def _():
        for dev in range(n_tm - 1):
            greet(dev)

    support = sup_in[0]
    lane = lax.broadcasted_iota(jnp.int32, (8, half), 1)
    loads = [pltpu.make_async_copy(pts_hbm.at[0, :, 0:half], pts.at[q, 0:dim], lsem.at[0]),
             pltpu.make_async_copy(pts_hbm.at[0, :, half:2 * half], pts2.at[0:dim], lsem.at[1]),
             pltpu.make_async_copy(pot_hbm, pot_in, lsem.at[2])]
    for c in loads:
        c.start()
    pts[q, dim:dim + 8, :] = (lane < support).astype(F32)
    pts2[dim:dim + 8, :] = (lane + half < support).astype(F32)
    loads[0].wait()
    loads[1].wait()
    peers = (TEAM - 1 + jnp.where(is_first, 0, 1) + jnp.where(is_last, 0, 1)
             + jnp.where(me == last, n_tm - 1, 1))
    pl.semaphore_wait(barrier, peers)

    to_sib = rc(pts.at[q], pts.at[q], S_PT, R_PT + q, sib)
    to_ymate = rc(pts.at[q], pts.at[q], S_PT + 1, R_PT + q, ymate)
    to_sib.start()
    head = [rc(pts2, pts.at[TEAM], S_GA + 2, R_PRED, 1),
            rc(potb, gat, S_GA, R_GA, 1),
            rc(potb2, gat2, S_GA + 1, R_GA + 1, 1)]

    @pl.when(me == 0)
    def _():
        head[0].start()

    @pl.when(me != 0)
    def _():
        to_ymate.start()

    loads[2].wait()
    for b in range(TEAM):
        potb[b] = pot_in[0, starts[b]:starts[b] + ROWS, 0:half].astype(BF16)

    @pl.when(me == 0)
    def _():
        for b in range(TEAM):
            potb2[b] = pot_in[0, starts[b]:starts[b] + ROWS, half:2 * half].astype(BF16)

    @pl.when(me == 0)
    def _():
        head[1].start()
        head[2].start()

    sends_pot = jnp.logical_or(inner, q >= 2)
    pot_copies = []
    for d in range(1, TEAM):
        mq = lax.rem(q + d, TEAM)
        pot_copies.append(rc(potb.at[mq], potr.at[q], S_POT + d - 1, R_POT + q, base + mq))

    @pl.when(sends_pot)
    def _():
        for c in pot_copies:
            c.start()

    potr[q] = potb[q]

    def recv_points(slot):
        rc(pts.at[slot], pts.at[slot], S_PT, R_PT + slot, me).wait_recv()

    unit = math.log2(math.e) / (2.0 * EPS_SCALE * dim)

    def generate(src, dst, res):
        x = src[0:dim, :]
        y = dst[0:dim, :]
        live = dst[dim:dim + 1, :]
        u = (-unit * A_DECAY * A_DECAY) * jnp.sum(x * x, axis=0, keepdims=True)
        v = -unit * jnp.sum(y * y, axis=0, keepdims=True)
        v = jnp.where(live > 0.0, v, -1e9)
        row = lax.broadcasted_iota(jnp.int32, (dim, half), 0)
        uh, um, ul = split3(u)
        vh, vm, vl = split3(v)
        one = jnp.where(row < 6, 1.0, 0.0)
        xh, xl = split2(x)
        yh, yl = split2(y * (2.0 * A_DECAY * unit))
        opa[0:dim, :] = xh
        opa[dim:2 * dim, :] = xh
        opa[2 * dim:3 * dim, :] = xl
        opa[3 * dim:4 * dim, :] = jnp.where(
            row == 3, uh, jnp.where(row == 4, um, jnp.where(row == 5, ul, one))).astype(BF16)
        opb[0:dim, :] = yh
        opb[dim:2 * dim, :] = yl
        opb[2 * dim:3 * dim, :] = yh
        opb[3 * dim:4 * dim, :] = jnp.where(
            row == 0, vh, jnp.where(row == 1, vm, jnp.where(row == 2, vl, one))).astype(BF16)
        tile = 256

        @pl.loop(0, half // tile)
        def _(i):
            at = pl.ds(pl.multiple_of(i * tile, tile), tile)
            e = lax.dot_general(opa[:, at], opb[...], (((0,), (0,)), ((), ())),
                                preferred_element_type=F32)
            res[at, :] = jnp.exp2(e).astype(BF16)

    def log_row(value):
        spread = jnp.broadcast_to(value, (ROWS, 128))
        r0 = lax.broadcasted_iota(jnp.int32, (ROWS, 128), 0)
        r1 = lax.broadcasted_iota(jnp.int32, (ROWS, 128), 1)
        return jnp.sum(jnp.where(r0 == r1, spread, 0.0), axis=0, keepdims=True)

    def count(ref):
        return jnp.sum(ref[dim:dim + 1, :], axis=1, keepdims=True)

    def blocks(ref):
        return ref[...].reshape(TEAM * ROWS, half)

    w1_copies = []
    for d in range(1, TEAM):
        mq = lax.rem(1 + d, TEAM)
        w1_copies.append((rc(w1.at[mq], wbuf.at[2], S_W1 + d - 1, R_W, mq),
                          rc(log1.at[mq], logacc, S_L1 + d - 1, R_LW, mq)))

    recv_points(lax.rem(sib, TEAM))

    @pl.when(me == 1)
    def _():
        head[0].wait_recv()
        generate(pts.at[0], pts.at[1], kern.at[1])
        generate(pts.at[TEAM], pts.at[1], kern.at[0])
        head[1].wait_recv()
        head[2].wait_recv()
        pushed = (jnp.dot(blocks(gat), kern[1], preferred_element_type=F32)
                  + jnp.dot(blocks(gat2), kern[0], preferred_element_type=F32))
        cs = jnp.sum(pushed, axis=1, keepdims=True)
        cnt = count(pts.at[1])
        push[:, 0:half] = pushed * (cnt / cs)
        for b in (2, 3, 0, 1):
            rows = slice(starts[b], starts[b] + ROWS)
            m = push[b * ROWS:(b + 1) * ROWS, 0:half]
            w = (m * pot_in[0, rows, 0:half]).astype(BF16)
            if b == 1:
                wbuf[2] = w
            else:
                w1[b] = w
                w1_copies[(b + 2) % TEAM][0].start()
        for b in range(TEAM):
            lr = log_row(jnp.log(cs[b * ROWS:(b + 1) * ROWS] / cnt))
            if b == 1:
                logacc[...] = jnp.broadcast_to(lr, logacc.shape)
            else:
                log1[b] = jnp.broadcast_to(lr, logacc.shape)
                w1_copies[(b + 2) % TEAM][1].start()
        for b in range(TEAM):
            out[0, starts[b]:starts[b] + ROWS, 0:half] = push[b * ROWS:(b + 1) * ROWS, 0:half]

    forward = rc(pts.at[yq], pts.at[yq], S_PT + 2, R_PT + yq, sib)
    diag = lax.rem(lax.rem(sib, TEAM) + 2, TEAM)

    @pl.when(me != 2)
    def _():
        recv_points(yq)
        forward.start()

    @pl.when(me != 3)
    def _():
        recv_points(diag)

    pred = rc(pts.at[TEAM - 1], pts.at[TEAM], S_PRED, R_PRED, me + TEAM)

    @pl.when(jnp.logical_not(is_last))
    def _():
        pred.start()

    generate(pts.at[1], pts.at[2], kern.at[2])

    @pl.when(jnp.logical_or(jnp.logical_not(is_last), q == TEAM - 1))
    def _():
        generate(pts.at[2], pts.at[3], kern.at[3])

    @pl.when(me == last)
    def _():
        generate(pts.at[2], pts2, kern2)

    @pl.when(inner)
    def _():
        generate(pts.at[0], pts.at[1], kern.at[1])
        pred.wait_recv()
        generate(pts.at[TEAM], pts.at[0], kern.at[0])

    w_in = rc(wbuf.at[TEAM], wbuf.at[0], S_W, R_W, me + TEAM)
    l_in = rc(logacc, logacc, S_LW, R_LW, me + TEAM)

    @pl.when(me != 1)
    def _():
        w_in.wait_recv()
        l_in.wait_recv()

    to_owner = [rc(wbuf.at[s], gat.at[q], S_G + s, R_G + q, base + s) for s in range(TEAM)]

    def offer(s):
        @pl.when(q == s)
        def _():
            gat[q] = wbuf[s]

        @pl.when(q != s)
        def _():
            to_owner[s].start()

    def step(s):
        if s == 2:
            @pl.when(jnp.logical_not(is_last))
            def _():
                offer(s)
        else:
            offer(s)

        pushed = jnp.dot(wbuf[s], kern[s], preferred_element_type=F32)
        cs = jnp.sum(pushed, axis=1, keepdims=True)
        cnt = count(pts.at[s])

        @pl.when(q != s)
        def _():
            rc(potr.at[s], potr.at[s], S_POT, R_POT + s, me).wait_recv()

        wbuf[s + 1] = (pushed * (cnt / cs) * potr[s].astype(F32)).astype(BF16)
        if s == TEAM - 1:
            w_in.start()
        logacc[...] += jnp.broadcast_to(log_row(jnp.log(cs / cnt)), logacc.shape)

    @pl.when(inner)
    def _():
        step(0)
        step(1)

    step(2)

    l_gat = rc(logacc, loggat.at[q], S_LG, R_LG + q, last)

    @pl.when(jnp.logical_not(is_last))
    def _():
        step(3)
        l_in.start()

    @pl.when(is_last)
    def _():
        offer(3)

        @pl.when(me != last)
        def _():
            l_gat.start()
            to_owner[3].wait_send()

        offer(2)

        @pl.when(me != last)
        def _():
            rc(potr.at[3], potr.at[3], S_POT, R_POT + 3, me).wait_recv()

        @pl.when(me == last)
        def _():
            loggat[q] = logacc[...]

    @pl.when(jnp.logical_or(inner, q >= 2))
    def _():
        for d in range(1, TEAM):
            mq = lax.rem(q + d, TEAM)
            rc(gat.at[mq], gat.at[mq], S_G, R_G + mq, me).wait_recv()

    @pl.when(me == 0)
    def _():
        full = lax.broadcasted_iota(jnp.int32, (cols, 2 * half), 1)
        out[0] = (full < support).astype(F32)

    @pl.when(jnp.logical_and(me != 0, me != last))
    def _():
        out[0, :, half:2 * half] = jnp.zeros((cols, half), F32)

    @pl.when(jnp.logical_and(jnp.logical_or(inner, q >= 2), me != last))
    def _():
        pushed = jnp.dot(blocks(gat), kern[q], preferred_element_type=F32)
        cs = jnp.sum(pushed, axis=1, keepdims=True)
        push[:, 0:half] = pushed * (count(pts.at[q]) / cs)
        for b in range(TEAM):
            out[0, starts[b]:starts[b] + ROWS, 0:half] = push[b * ROWS:(b + 1) * ROWS, 0:half]

    fin = [rc(logfin, logfin, S_FIN + dev, R_FIN, dev) for dev in range(n_tm - 1)]

    @pl.when(me == last)
    def _():
        pa = jnp.dot(blocks(gat), kern[TEAM - 1], preferred_element_type=F32)
        pb = jnp.dot(blocks(gat), kern2[...], preferred_element_type=F32)
        cs = jnp.sum(pa, axis=1, keepdims=True) + jnp.sum(pb, axis=1, keepdims=True)
        cnt = count(pts.at[TEAM - 1]) + count(pts2)
        term = jnp.log(cs / cnt)
        for b in range(TEAM - 1):
            rc(loggat.at[b], loggat.at[b], S_LG, R_LG + b, me).wait_recv()
        logfin[...] = jnp.zeros_like(logfin)
        for b in range(TEAM):
            total = loggat[b, 0:1, :] + log_row(term[b * ROWS:(b + 1) * ROWS])
            logfin[b:b + 1, :] = total * (1.0 / (n_tm - 1))
        for c in fin:
            c.start()
        push[:, 0:half] = pa * (cnt / cs)
        push[:, half:2 * half] = pb * (cnt / cs)
        for b in range(TEAM):
            out[0, starts[b]:starts[b] + ROWS, :] = push[b * ROWS:(b + 1) * ROWS, :]
        for c in fin:
            c.wait_send()

    to_sib.wait_send()

    @pl.when(me != 0)
    def _():
        to_ymate.wait_send()

    @pl.when(me != 2)
    def _():
        forward.wait_send()

    @pl.when(me == 0)
    def _():
        for c in head:
            c.wait_send()

    @pl.when(me == 1)
    def _():
        for a, b in w1_copies:
            a.wait_send()
            b.wait_send()

    @pl.when(sends_pot)
    def _():
        for c in pot_copies:
            c.wait_send()

    @pl.when(jnp.logical_not(is_last))
    def _():
        pred.wait_send()
        w_in.wait_send()
        l_in.wait_send()

    for s in range(TEAM):
        sent = jnp.logical_and(q != s, jnp.logical_or(inner, s >= 2))
        if s == 3:
            sent = jnp.logical_and(sent, jnp.logical_not(is_last))

        @pl.when(sent)
        def _(s=s):
            to_owner[s].wait_send()

    @pl.when(jnp.logical_and(is_last, me != last))
    def _():
        l_gat.wait_send()

    @pl.when(me != last)
    def _():
        rc(logfin, logfin, S_FIN, R_FIN, me).wait_recv()

    logout[...] = logfin[...]


def per_device(n_tm, points, potentials, supports):
    slices, dim, count = points.shape
    cols = potentials.shape[1]
    half = count // 2
    starts = [(b * (cols - ROWS) // (TEAM - 1)) // 16 * 16 for b in range(TEAM)]
    vm = lambda shape, dtype: pltpu.VMEM(shape, dtype)
    messages, logs = pl.pallas_call(
        functools.partial(kernel, n_tm, starts, half),
        out_shape=(jax.ShapeDtypeStruct((slices, cols, count), F32),
                   jax.ShapeDtypeStruct((8, 128), F32)),
        in_specs=[pl.BlockSpec(memory_space=pltpu.HBM),
                  pl.BlockSpec(memory_space=pltpu.HBM),
                  pl.BlockSpec(memory_space=pltpu.SMEM)],
        out_specs=(pl.BlockSpec(memory_space=pltpu.VMEM),
                   pl.BlockSpec(memory_space=pltpu.VMEM)),
        scratch_shapes=[
            vm((TEAM + 1, dim + 8, half), F32),
            vm((dim + 8, half), F32),
            vm((TEAM, ROWS, half), BF16),
            vm((TEAM, ROWS, half), BF16),
            vm((TEAM, ROWS, half), BF16),
            vm((TEAM, half, half), BF16),
            vm((half, half), BF16),
            vm((4 * dim, half), BF16),
            vm((4 * dim, half), BF16),
            vm((TEAM + 1, ROWS, half), BF16),
            vm((TEAM, ROWS, half), BF16),
            vm((TEAM, ROWS, half), BF16),
            vm((TEAM, ROWS, half), BF16),
            vm((TEAM * ROWS, 2 * half), F32),
            vm((8, 128), F32),
            vm((TEAM, 8, 128), F32),
            vm((TEAM, 8, 128), F32),
            vm((8, 128), F32),
            vm((slices, cols, count), F32),
            pltpu.SemaphoreType.DMA((S_FIN + n_tm,)),
            pltpu.SemaphoreType.DMA((N_RECV,)),
            pltpu.SemaphoreType.DMA((3,)),
        ],
        compiler_params=pltpu.CompilerParams(
            collective_id=0, has_side_effects=True, vmem_limit_bytes=62 * 1024 * 1024),
    )(points, potentials, supports)
    ends = starts[1:] + [cols]
    log_scale = jnp.concatenate(
        [logs[b, 0:ends[b] - starts[b]] for b in range(TEAM)])
    return messages, log_scale


def solution(mesh):
    placed = (P(("groups", "tm"), None, None), P(("groups", "tm"), None, None), P(("groups", "tm")))
    return jax.shard_map(
        functools.partial(per_device, mesh.shape["tm"]),
        mesh=mesh,
        in_specs=placed,
        out_specs=(P(("groups", "tm"), None, None), P("groups")),
        check_vma=False,
    )
```
